32 devices in a mesh: scan: 4 (over y, x), det: 8 (over z, core).
Axes of the slice: x: 2, y: 2, z: 4, core: 2. Of those that a mesh axis runs over, the one named last changes fastest.
Arguments:
- data: float32 [2, 512, 2, 256, 256], P(None, 'scan', None, 'det'), may hold values from -6 to 6
- wigner: float32 [2, 512, 2, 256, 256], P(None, ('scan', 'det')), may hold values from -6 to 6
Outputs:
- deconvolved: float32 [2, 512, 2, 256, 256], P(None, 'scan', None, 'det')
The draws below stay inside these ranges and needn't reach their ends.
All inputs are finite; a program needn't handle non-finite values.
Results may differ from the reference program's by a relative error of at most 0.0001.
Values sent between devices are 32-bit elements; how exact they have to be, the bound alone decides.
A program may use at most 192 MiB of HBM per device.

```python
import math
import jax
import jax.numpy as jnp

SR = 512
DET = 256
FREQS = 2


def shard_levels(key, shape, split, smallest, top_value):
    def one(position, blocks):
        draws = jax.random.uniform(jax.random.fold_in(jax.random.fold_in(key, 6), position), (blocks,), jnp.float32, smallest / len(split), top_value / len(split))
        return jnp.repeat(jnp.exp(draws), shape[position] // blocks).reshape((-1,) + (1,) * (len(shape) - position - 1))

    level = one(*split[0])
    for cut in split[1:]:
        level = level * one(*cut)
    return level


def scatter_about(own_key, dims, scale, limit, cuts=(), held_as=jnp.bfloat16):
    result = jax.random.normal(own_key, dims, jnp.float32) * scale
    if len(cuts) > 0:
        result = shard_levels(own_key, dims, cuts, -0.22, 0.18) * result
    return jnp.clip(result, min=-limit, max=limit).astype(held_as)


def setup_inputs(seed: int = 0) -> dict:
    key_list = jax.random.split(jax.random.key(seed), 3)
    data = scatter_about(key_list[0], (2, SR, FREQS, DET, DET), 1.0, 6.0, ((1, 4), (3, 8)), jnp.float32)
    wigner = scatter_about(key_list[1], (2, SR, FREQS, DET, DET), 1.0, 6.0, ((1, 32),), jnp.float32)
    return {"data": data, "wigner": wigner}


eps_wiener = 0.1

def reference(data, wigner):
    results = []
    for freq_index in range(FREQS):
        planes = data[0, :, freq_index] + 1j * data[1, :, freq_index]
        spectra = jnp.fft.fft(planes, axis=0) / math.sqrt(SR)
        spatial = jnp.fft.ifft2(spectra, axes=(1, 2)) * DET
        kernel = (wigner[0, :, freq_index] + 1j * wigner[1, :, freq_index]).transpose(0, 2, 1)
        power = kernel.real * kernel.real + kernel.imag * kernel.imag + eps_wiener
        filtered = spatial * jnp.conj(kernel) / power
        output_planes = jnp.fft.fft2(filtered, axes=(1, 2)) / DET
        results.append(jnp.stack([output_planes.real, output_planes.imag]).astype(jnp.float32))
    return jnp.stack(results, axis=2)
```

```python
import functools
import math

import jax
import jax.numpy as jnp
import ml_dtypes
import numpy as np
from jax import lax
from jax.experimental import pallas as pl
from jax.experimental.pallas import tpu as pltpu
from jax.sharding import PartitionSpec as P

eps_wiener = 0.1


def tables(count, sign):
    indices = jnp.arange(count, dtype=jnp.int32)
    product = indices[:, None] * indices[None, :] % count
    phases = product.astype(jnp.float32) * (2.0 * math.pi / count)
    norm_scale = 1.0 / math.sqrt(count)
    return (jnp.cos(phases) * norm_scale, sign * jnp.sin(phases) * norm_scale)


def product_form(form, left, right):
    return jnp.einsum(form, left, right, precision=lax.Precision.HIGHEST)


def pair_right(real_in, imag_in, form, cosine, sines):
    real_out = product_form(form, real_in, cosine) - product_form(form, imag_in, sines)
    imag_out = product_form(form, real_in, sines) + product_form(form, imag_in, cosine)
    return (real_out, imag_out)


def pair_left(cosine, sines, real_in, imag_in):
    real_out = jnp.dot(cosine, real_in, precision=lax.Precision.HIGHEST) - jnp.dot(
        sines, imag_in, precision=lax.Precision.HIGHEST
    )
    imag_out = jnp.dot(cosine, imag_in, precision=lax.Precision.HIGHEST) + jnp.dot(
        sines, real_in, precision=lax.Precision.HIGHEST
    )
    return (real_out, imag_out)


def shards_plain(data, wigner):
    detector = data.shape[4]
    freq_count = data.shape[2]
    local_rows = data.shape[3]
    rows_total = data.shape[1] * lax.axis_size("scan")
    inv_cos, inv_sin = tables(detector, 1.0)
    fwd_cos, fwd_sin = tables(detector, -1.0)
    row_cos, row_sin = tables(rows_total, -1.0)
    space_real, space_imag = pair_right(data[0], data[1], "rfab,by->rfay", inv_cos, inv_sin)
    flat_cols = freq_count * local_rows * detector
    space_real = space_real.reshape(data.shape[1], flat_cols)
    space_imag = space_imag.reshape(data.shape[1], flat_cols)
    whole_real, whole_imag = (
        lax.all_to_all(space_real, "scan", split_axis=1, concat_axis=0, tiled=True),
        lax.all_to_all(space_imag, "scan", split_axis=1, concat_axis=0, tiled=True),
    )
    spec_real, spec_imag = pair_left(row_cos, row_sin, whole_real, whole_imag)
    back_real, back_imag = (
        lax.all_to_all(spec_real, "scan", split_axis=0, concat_axis=1, tiled=True),
        lax.all_to_all(spec_imag, "scan", split_axis=0, concat_axis=1, tiled=True),
    )
    block_freqs = back_real.shape[0]
    back_real = back_real.reshape(block_freqs, freq_count, local_rows, detector)
    back_imag = back_imag.reshape(block_freqs, freq_count, local_rows, detector)
    field_real, field_imag = pair_right(
        lax.all_to_all(back_real, "det", split_axis=0, concat_axis=2, tiled=True),
        lax.all_to_all(back_imag, "det", split_axis=0, concat_axis=2, tiled=True),
        "qfay,xa->qfyx",
        inv_cos,
        inv_sin,
    )
    kernel_real = wigner[0]
    kernel_imag = wigner[1]
    power = kernel_real * kernel_real + kernel_imag * kernel_imag + eps_wiener
    filtered_real = (field_real * kernel_real + field_imag * kernel_imag) / power
    filtered_imag = (field_imag * kernel_real - field_real * kernel_imag) / power
    half_real, half_imag = pair_right(
        filtered_real, filtered_imag, "qfyx,ax->qfya", fwd_cos, fwd_sin
    )
    plane_real, plane_imag = pair_right(half_real, half_imag, "qfya,by->qfab", fwd_cos, fwd_sin)
    final_real, final_imag = (
        lax.all_to_all(plane_real, "det", split_axis=2, concat_axis=0, tiled=True),
        lax.all_to_all(plane_imag, "det", split_axis=2, concat_axis=0, tiled=True),
    )
    return jnp.stack([final_real, final_imag])


LANES = 128
PARAMS = pltpu.CompilerParams(vmem_limit_bytes=40 * 1024 * 1024)


def phases(left, right, count, sign):
    angle = 2.0 * math.pi / count * (np.outer(left, right) % count)
    scale = 1.0 / math.sqrt(count)
    return np.cos(angle) * scale, sign * np.sin(angle) * scale


def halves(table):
    table = table.astype(np.float32)
    high = table.astype(ml_dtypes.bfloat16)
    low = (table - high.astype(np.float32)).astype(ml_dtypes.bfloat16)
    return jnp.asarray(high), jnp.asarray(low)


def right_table(left, right, count, sign):
    real, imag = phases(left, right, count, sign)
    return halves(np.block([[real, imag], [-imag, real]]))


def split(value):
    high = value.astype(jnp.bfloat16)
    low = (value - high.astype(jnp.float32)).astype(jnp.bfloat16)
    return high, low


def dot(left, right):
    return jnp.dot(left, right, preferred_element_type=jnp.float32)


def times(value, high, low):
    value_high, value_low = split(value)
    return dot(value_high, high) + (dot(value_low, high) + dot(value_high, low))


def column_kernel(me, data, high, low, out):
    _, rows, _, group, detector = data.shape
    both = jnp.concatenate(
        [data[c, :, 0].reshape(rows * group, detector) for c in range(2)], axis=1
    )
    result = times(both, high[...], low[...])
    for c in range(2):
        part = result[:, c * LANES : (c + 1) * LANES].reshape(rows, group, LANES)
        out[0, c] = jnp.swapaxes(part, 0, 1)


def columns_to_space(me, data, freq, table, parts):
    _, rows, _, local_rows, detector = data.shape
    group = local_rows // parts
    flops = 2 * 3 * rows * local_rows * 2 * detector * 2 * LANES
    return pl.pallas_call(
        column_kernel,
        grid_spec=pltpu.PrefetchScalarGridSpec(
            num_scalar_prefetch=1,
            grid=(parts,),
            in_specs=[
                pl.BlockSpec(
                    (2, rows, 1, group, detector),
                    lambda i, me: (0, 0, freq, jnp.bitwise_xor(i, me[0]), 0),
                ),
                pl.BlockSpec((2 * detector, 2 * LANES), lambda i, me: (0, 0)),
                pl.BlockSpec((2 * detector, 2 * LANES), lambda i, me: (0, 0)),
            ],
            out_specs=pl.BlockSpec((1, 2, group, rows, LANES), lambda i, me: (i, 0, 0, 0, 0)),
        ),
        out_shape=jax.ShapeDtypeStruct((parts, 2, group, rows, LANES), jnp.float32),
        compiler_params=PARAMS,
        cost_estimate=pl.CostEstimate(
            flops=flops, bytes_accessed=12 * 2 * rows * local_rows * LANES, transcendentals=0
        ),
        name="columns_to_space",
    )(me, data, *table)


def row_kernel(me, *refs):
    sources, (high, low, out, held_high, held_low) = refs[:-5], refs[-5:]
    parts = len(sources)
    _, group, rows, _ = sources[0].shape
    _, block, total = high.shape
    dests, _, share, _, _ = out.shape

    @pl.when(pl.program_id(0) == 0)
    def _():
        for c in range(2):
            for s in range(parts):
                sender = jnp.bitwise_xor(me[0], s)
                at = pl.ds(pl.multiple_of((c * parts + sender) * rows, rows), rows)
                for a in range(group):
                    piece_high, piece_low = split(sources[s][c, a])
                    held_high[at, a * LANES : (a + 1) * LANES] = piece_high
                    held_low[at, a * LANES : (a + 1) * LANES] = piece_low

    for c in range(2):
        result = dot(high[c], held_high[...]) + (
            dot(high[c], held_low[...]) + dot(low[c], held_high[...])
        )
        stacked = jnp.stack(
            [result[:, a * LANES : (a + 1) * LANES] for a in range(group)], axis=1
        )
        out[:, c] = stacked.reshape(dests, share, group, LANES)


def rows_to_freqs(me, sources, table, devices, steps):
    parts = len(sources)
    _, group, rows, _ = sources[0].shape
    total = parts * rows
    share = total // devices
    return pl.pallas_call(
        row_kernel,
        grid=(steps,),
        in_specs=[
            pl.BlockSpec(memory_space=pltpu.SMEM),
            *(pl.BlockSpec(source.shape, lambda i: (0, 0, 0, 0)) for source in sources),
            pl.BlockSpec((2, total // steps, 2 * total), lambda i: (0, i, 0)),
            pl.BlockSpec((2, total // steps, 2 * total), lambda i: (0, i, 0)),
        ],
        out_specs=pl.BlockSpec(
            (devices // steps, 2, share, group, LANES), lambda i: (i, 0, 0, 0, 0)
        ),
        out_shape=jax.ShapeDtypeStruct((devices, 2, share, group, LANES), jnp.float32),
        scratch_shapes=[pltpu.VMEM((2 * total, group * LANES), jnp.bfloat16)] * 2,
        compiler_params=PARAMS,
        cost_estimate=pl.CostEstimate(
            flops=2 * 3 * 4 * total * total * group * LANES,
            bytes_accessed=16 * total * group * LANES,
            transcendentals=0,
        ),
        name="rows_to_freqs",
    )(me, *sources, *table)


def filter_kernel(source, wigner, there_high, there_low, back_high, back_low, out):
    devices, _, batch, group, _ = source.shape
    dests, _, _, local_rows, _ = out.shape
    detector = devices * group
    planes = []
    for q in range(batch):
        plane = jnp.concatenate(
            [source[:, c, q].reshape(detector, LANES) for c in range(2)], axis=0
        )
        planes.append(jnp.transpose(plane))
    field = times(jnp.concatenate(planes, axis=0), there_high[...], there_low[...])
    field_real, field_imag = field[:, :detector], field[:, detector:]
    kernel_real = wigner[0, :, 0].reshape(batch * LANES, detector)
    kernel_imag = wigner[1, :, 0].reshape(batch * LANES, detector)
    power = kernel_real * kernel_real + kernel_imag * kernel_imag + eps_wiener
    inverse = 1.0 / power
    filtered = jnp.concatenate(
        [
            (field_real * kernel_real + field_imag * kernel_imag) * inverse,
            (field_imag * kernel_real - field_real * kernel_imag) * inverse,
        ],
        axis=1,
    )
    result = times(filtered, back_high[...], back_low[...])
    for q in range(batch):
        plane = jnp.transpose(result[q * LANES : (q + 1) * LANES])
        for c in range(2):
            part = plane[c * detector : (c + 1) * detector]
            out[:, c, q] = part.reshape(dests, local_rows, LANES)


def filter_planes(source, wigner, freq, chunk, there, back, dests, batch):
    devices, _, share, group, _ = source.shape
    detector = devices * group
    local_rows = detector // dests
    whole = pl.BlockSpec((2 * detector, 2 * detector), lambda i: (0, 0))
    return pl.pallas_call(
        filter_kernel,
        grid=(share // batch,),
        in_specs=[
            pl.BlockSpec((devices, 2, batch, group, LANES), lambda i: (0, 0, i, 0, 0)),
            pl.BlockSpec((2, batch, 1, LANES, detector), lambda i: (0, i, freq, chunk, 0)),
            whole,
            whole,
            whole,
            whole,
        ],
        out_specs=pl.BlockSpec((dests, 2, batch, local_rows, LANES), lambda i: (0, 0, i, 0, 0)),
        out_shape=jax.ShapeDtypeStruct((dests, 2, share, local_rows, LANES), jnp.float32),
        compiler_params=PARAMS,
        cost_estimate=pl.CostEstimate(
            flops=2 * 2 * 3 * 4 * share * LANES * detector * detector,
            bytes_accessed=24 * share * LANES * detector,
            transcendentals=0,
        ),
        name="filter_planes",
    )(source, wigner, *there, *back)


def final_kernel(*refs):
    sources, (high, low), out = refs[:-3], refs[-3:-1], refs[-1]
    _, _, share, local_rows, _ = sources[0].shape
    detector = out.shape[4]
    rows = share * local_rows
    both = jnp.concatenate(
        [piece[0, c].reshape(rows, LANES) for c in range(2) for piece in sources], axis=1
    )
    result = times(both, high[...], low[...])
    for c in range(2):
        part = result[:, c * detector : (c + 1) * detector]
        out[c, :, 0] = part.reshape(share, local_rows, detector)


def space_to_columns(sources, freq, freq_count, table, held):
    dests, _, share, local_rows, _ = sources[0].shape
    detector = len(sources) * LANES
    whole = pl.BlockSpec((2 * detector, 2 * detector), lambda i: (0, 0))
    in_specs = [
        pl.BlockSpec((1, 2, share, local_rows, LANES), lambda i: (i, 0, 0, 0, 0)) for _ in sources
    ] + [whole, whole]
    args = list(sources) + list(table)
    body = final_kernel
    aliases = {}
    if held is not None:
        in_specs = [pl.BlockSpec(memory_space=pl.ANY)] + in_specs
        args = [held] + args
        aliases = {0: 0}
        body = lambda *refs: final_kernel(*refs[1:])
    return pl.pallas_call(
        body,
        grid=(dests,),
        in_specs=in_specs,
        out_specs=pl.BlockSpec((2, share, 1, local_rows, detector), lambda i: (0, i, freq, 0, 0)),
        out_shape=jax.ShapeDtypeStruct(
            (2, dests * share, freq_count, local_rows, detector), jnp.float32
        ),
        input_output_aliases=aliases,
        compiler_params=PARAMS,
        cost_estimate=pl.CostEstimate(
            flops=2 * 3 * 4 * dests * share * local_rows * detector * detector,
            bytes_accessed=16 * dests * share * local_rows * detector,
            transcendentals=0,
        ),
        name="space_to_columns",
    )(*args)


def shards(data, wigner, scan, det):
    _, rows, freq_count, local_rows, detector = data.shape
    devices = scan * det
    group = local_rows // scan
    total = rows * scan
    points = np.arange(detector)
    chunks = detector // LANES
    spaces = [
        right_table(points, points[k * LANES : (k + 1) * LANES], detector, 1.0)
        for k in range(chunks)
    ]
    real, imag = phases(np.arange(total), np.arange(total), total, -1.0)
    row_table = tuple(
        part.reshape(2, total, 2 * total)
        for part in halves(np.block([[real, -imag], [imag, real]]))
    )
    arrival = points.reshape(det, scan, group).transpose(1, 0, 2).reshape(-1)
    there = right_table(arrival, points, detector, 1.0)
    back = right_table(points, points, detector, -1.0)

    me = lax.axis_index("scan").astype(jnp.int32).reshape(1)
    turn = me
    out = None
    for freq in range(freq_count):
        pieces = []
        for k in range(chunks):
            space = columns_to_space(turn, data, freq, spaces[k], scan)
            sources = [space[0]] + [
                lax.ppermute(space[i], "scan", [(j, j ^ i) for j in range(scan)])
                for i in range(1, scan)
            ]
            turn, sources = lax.optimization_barrier((turn, sources))
            spec = rows_to_freqs(me, sources, row_table, devices, scan)
            spec = lax.all_to_all(
                spec, ("scan", "det"), split_axis=0, concat_axis=0, tiled=True
            )
            plane = filter_planes(spec, wigner, freq, k, there, back, det, 2)
            pieces.append(lax.all_to_all(plane, "det", split_axis=0, concat_axis=0, tiled=True))
        out = space_to_columns(pieces, freq, freq_count, back, out)
    return out


def solution(mesh):
    in_specs = (P(None, "scan", None, "det", None), P(None, ("scan", "det"), None, None, None))
    out_specs = P(None, "scan", None, "det", None)
    scan, det = mesh.shape["scan"], mesh.shape["det"]

    def whole(data, wigner):
        detector = data.shape[4]
        share = data.shape[1] // (scan * det)
        tiled = detector % max(8 * scan * det, LANES) == 0 and share % 2 == 0 and scan & (scan - 1) == 0
        body = functools.partial(shards, scan=scan, det=det) if tiled else shards_plain
        return jax.shard_map(
            body, mesh=mesh, in_specs=in_specs, out_specs=out_specs, check_vma=False
        )(data, wigner)

    return whole
```
